256 devices in a mesh: rows: 64 (over z, y_lo, x), grp: 4 (over y_hi, core).
Axes of the slice: x: 4, y: 4 (y_hi: 2, y_lo: 2; y = y_hi * 2 + y_lo), z: 8, core: 2. Of those that a mesh axis runs over, the one named last changes fastest.
Arguments:
- tile_values: bfloat16 [8192, 16, 128], P('rows'), may hold values from 0.049804688 to 1
- tile_ids: int32 [8192, 16], P('rows'), may hold values from 0 to 255, as said below
- doc_tiles: int32 [8192], P('rows'), may hold values from 1 to 16
- row_counts: int32 [64], replicated, may hold values from 1 to 128, 4096 in all
Outputs:
- similarity: float32 [4096, 4096], P('rows', 'grp')
The draws below stay inside these ranges and needn't reach their ends.
Inputs may be any that keep to these rules, and one draw needn't show every extreme that they name: `row_counts`: the entries sum to 4096. `tile_ids`: the 16 entries of a row are distinct.
All inputs are finite; a program needn't handle non-finite values.
Results may differ from the reference program's by a relative error of at most 0.0003.
Values may be sent and summed in bfloat16 or wider, within the bound.
No kernel may reach another device: no remote copies, remote signals or barrier semaphores. Data moves between devices by JAX's collectives and lax.ppermute only.
A program may use at most 64 MiB of HBM per device.

```python
import math
import jax
import jax.numpy as jnp
import numpy as np
from jax import lax

VOCAB = 32768
TILE = 128
LTILES = 16
DOC_DEV = 64
PANELS = 64
CAP = 128
DOCS = 4096
N_ROWS = 64


def draw_doc_tiles(key, part):
    first_key, second_key = jax.random.split(jax.random.fold_in(key, 11))
    first_draw = jax.random.randint(first_key, (PANELS * CAP,), 1, LTILES + 1)
    second_draw = jax.random.randint(second_key, (PANELS * CAP,), 1, LTILES + 1)
    return jnp.maximum(first_draw, second_draw).astype(jnp.int32)


def draw_tile_ids(key, part):
    tile_count = VOCAB // TILE
    noise = jax.random.randint(jax.random.fold_in(key, 23), (PANELS * CAP, tile_count), 0, 4096)
    tile_rank = jnp.arange(tile_count, dtype=jnp.int32)
    scores = noise * (tile_rank + 8) * tile_count + tile_rank
    order = jnp.argsort(scores, axis=1)
    return order[:, :LTILES].astype(jnp.int32)


def level_of(stream_key, dims, cuts, least, top_value):
    def one(dim, parts):
        steps = jax.random.uniform(jax.random.fold_in(jax.random.fold_in(stream_key, 6), dim), (parts,), jnp.float32, least / len(cuts), top_value / len(cuts))
        return jnp.repeat(jnp.exp(steps), dims[dim] // parts).reshape((-1,) + (1,) * (len(dims) - dim - 1))

    level = one(*cuts[0])
    for cut in cuts[1:]:
        level = level * one(*cut)
    return level


def length_profile(amount, total, most, lean):
    loads = [(1 << 20) // math.isqrt(grade ** lean) + 1 for grade in range(2, amount + 1)]
    spare, given = total - most - (amount - 1), [1] * (amount - 1)
    while spare > 0:
        movable = [i for i in range(amount - 1) if given[i] < most]
        whole, left = sum([loads[i] for i in movable]), spare
        for i in movable:
            addition = min(most - given[i], max(1, left * loads[i] // whole), spare)
            given[i] = given[i] + addition
            spare = spare - addition
    return np.array([most] + given)


def uneven_parts(key, number_of, total, most, skew):
    if number_of == 2:
        one = jax.random.randint(key, (), max(1, total - most), min(most, total - 1) + 1)
        return jnp.stack([one, total - one])
    tallies = jnp.asarray(length_profile(number_of, total, most, skew), jnp.int32)
    couples = (number_of - 1) // 2
    source_of, sink = tallies[1:1 + 2 * couples:2], tallies[2:2 + 2 * couples:2]
    room = jnp.minimum(source_of - 1, most - sink)
    shifted = jax.random.randint(jax.random.fold_in(key, 1), (couples,), 0, 1 << 20) % (room + 1)
    tallies = tallies.at[1:1 + 2 * couples:2].set(source_of - shifted).at[2:2 + 2 * couples:2].set(sink + shifted)
    return tallies[jax.random.permutation(jax.random.fold_in(key, 2), number_of)]


def setup_inputs(seed: int = 0) -> dict:
    streams_of = jax.random.split(jax.random.key(seed), 5)
    return {
        "tile_values": jnp.clip(jnp.exp(math.log(1.0) - 2.9996462 * jax.random.uniform(streams_of[0], (PANELS * CAP, LTILES, TILE), jnp.float32) ** level_of(streams_of[0], (PANELS * CAP, LTILES, TILE), ((0, 64),), -0.2, 0.2)), 0.049804688, 1.0).astype(jnp.bfloat16),
        "tile_ids": draw_tile_ids(jax.random.fold_in(streams_of[4], 71), 0),
        "doc_tiles": draw_doc_tiles(jax.random.fold_in(streams_of[4], 71), 0),
        "row_counts": uneven_parts(streams_of[3], PANELS, DOCS, CAP, 2).astype(jnp.int32),
    }


def reference(tile_values, tile_ids, doc_tiles, row_counts):
    capacity = tile_values.shape[0] // N_ROWS
    live_mask = jnp.arange(LTILES, dtype=jnp.int32)[None, :] < doc_tiles[:, None]
    masked = jnp.where(live_mask[:, :, None], tile_values, jnp.zeros_like(tile_values))
    run_ends = jnp.cumsum(row_counts).astype(jnp.int32)
    run_starts = (run_ends - row_counts).astype(jnp.int32)
    position = jnp.arange(DOCS, dtype=jnp.int32)
    global_ids = ((position % DOC_DEV) * N_ROWS + position // DOC_DEV).astype(jnp.int32)
    source = jnp.searchsorted(run_ends, global_ids, side="right").astype(jnp.int32)
    slot_rows = (source * capacity + (global_ids - run_starts[source])).astype(jnp.int32)
    values = masked[slot_rows]
    codes = tile_ids[slot_rows]
    holder = jnp.zeros((DOCS, VOCAB // TILE, TILE), values.dtype)
    holder = holder.at[jnp.arange(DOCS, dtype=jnp.int32)[:, None], codes].set(values)
    dense = holder.reshape(DOCS, VOCAB)
    widened = values.astype(jnp.float32)
    norms = jnp.sum(widened * widened, axis=(1, 2))

    def panel(panel_index):
        rows_here = lax.dynamic_slice_in_dim(dense, panel_index * DOC_DEV, DOC_DEV, 0)
        norms_here = lax.dynamic_slice_in_dim(norms, panel_index * DOC_DEV, DOC_DEV, 0)
        product = jnp.dot(rows_here, dense.T, preferred_element_type=jnp.float32)
        ratio = product / (norms_here[:, None] + norms[None, :] - product)
        order = ((panel_index - jnp.arange(N_ROWS, dtype=jnp.int32)) % N_ROWS).astype(jnp.int32)
        return ratio.reshape(DOC_DEV, N_ROWS, DOC_DEV)[:, order, :].reshape(DOC_DEV, DOCS)

    result = lax.map(panel, jnp.arange(N_ROWS, dtype=jnp.int32))
    return result.reshape(DOCS, DOCS)
```

```python
import jax
import jax.numpy as jnp
from jax import lax
from jax.experimental import pallas as pl
from jax.experimental.pallas import tpu as pltpu
from jax.sharding import Mesh
from jax.sharding import PartitionSpec as P

TILES = 16
LANES = 128
SENT = 24
PIECE = TILES + 1
BF16 = jnp.bfloat16
F32 = jnp.float32
VMEM = pl.BlockSpec(memory_space=pltpu.VMEM)
SMEM = pl.BlockSpec(memory_space=pltpu.SMEM)


def params(mib):
    return pltpu.CompilerParams(vmem_limit_bytes=mib * 2**20)


def pack_kernel(counts, tiles, ids, values, out, source, wide_ids):
    z, yl, x = lax.axis_index("z"), lax.axis_index("yl"), lax.axis_index("x")
    yh, c = lax.axis_index("yh"), lax.axis_index("c")
    here = z * 8 + yl * 4 + x
    base = (yh * 2 + yl) * 64 + z * 8 + c * 4 + x

    def scan(e, carry):
        begin, own_begin = carry
        end = begin + counts[e]
        number = begin + ((base - begin) & 255)

        @pl.when(number < end)
        def _():
            source[number >> 8] = e

        return end, jnp.where(e == here, begin, own_begin)

    _, own_begin = lax.fori_loop(0, 64, scan, (jnp.int32(0), jnp.int32(0)), unroll=8)
    wide_ids[...] = jnp.zeros_like(wide_ids)
    wide_ids[:, 0:TILES] = ids[...].astype(F32)
    tile_line = lax.broadcasted_iota(jnp.int32, (TILES, LANES), 0)

    def fill(t, carry):
        wanted = (yh * 2 + ((t >> 2) & 1)) * 64 + (t >> 3) * 8 + c * 4 + (t & 3)
        slot = jnp.minimum((wanted - own_begin) & 255, 127)
        document = jnp.where(tile_line < tiles[slot], values[slot].astype(F32), 0.0)
        codes = jnp.broadcast_to(wide_ids[pl.ds(slot, 1), :], (SENT - TILES, LANES))
        out[t] = jnp.concatenate([document, codes], axis=0).astype(BF16)
        return carry

    lax.fori_loop(0, 64, fill, 0, unroll=8)


def arrange_kernel(source, arrived, piece, spread, lines):
    for m in range(16):
        lines[pl.ds(m * SENT, SENT), :] = arrived[source[m]].astype(F32)
    total = jnp.zeros((16, LANES), F32)
    parts = []
    for k in range(TILES):
        part = lines[pl.ds(k, 16, stride=SENT), :]
        total = total + part * part
        parts.append(part.astype(BF16))
    norms = jnp.sum(total, axis=1, keepdims=True)
    high = norms.astype(BF16).astype(F32)
    middle = (norms - high).astype(BF16).astype(F32)
    low = norms - high - middle
    lane = lax.broadcasted_iota(jnp.int32, (16, LANES), 1)
    codes = lines[pl.ds(TILES, 16, stride=SENT), :]
    codes = jnp.where(lane == 16, high, codes)
    codes = jnp.where(lane == 17, middle, codes)
    codes = jnp.where(lane == 18, low, codes)
    parts.append(codes.astype(BF16))
    whole = jnp.concatenate([part[None] for part in parts], axis=0)
    piece[...] = whole
    for j in range(16):
        spread[j] = whole


def compare_kernel(rows, own, other, out, columns, column_codes, row_codes, row_norms, acc):
    x, c = lax.axis_index("x"), lax.axis_index("c")
    for u in range(16):
        part = own[u // 2] if u % 2 == 0 else other[((u + 1) // 2 - c) & 7]
        for k in range(TILES):
            columns[k, u * 16 : (u + 1) * 16, :] = part[k]
        column_codes[u * 16 : (u + 1) * 16, :] = part[TILES].astype(F32)
    across = jnp.transpose(column_codes[...], (1, 0))
    column_codes[0:128, :] = across[:, 0:128]
    column_codes[128:256, :] = across[:, 128:256]
    norms_across = across[16:17] + across[17:18] + across[18:19]
    for j in range(16):
        codes = rows[j, TILES].astype(F32)
        for k in range(TILES):
            row_codes[j, k] = jnp.broadcast_to(codes[:, k : k + 1], (16, LANES))
        norms = codes[:, 16:17] + codes[:, 17:18] + codes[:, 18:19]
        row_norms[j] = jnp.broadcast_to(norms, (16, LANES))
    acc[...] = jnp.zeros_like(acc)

    @pl.loop(0, 8)
    def _(pair):
        for b in (2 * pair, 2 * pair + 1):
            weights = jnp.transpose(columns[b], (1, 0))
            codes_b = jnp.concatenate(
                [column_codes[pl.ds(b, 1), :], column_codes[pl.ds(128 + b, 1), :]], axis=1
            )
            for j in range(16):
                left = rows[j, 0:TILES].reshape(256, LANES)
                product = jnp.dot(left, weights, preferred_element_type=F32)
                codes_j = row_codes[j].reshape(256, LANES)
                same = jnp.concatenate([codes_j, codes_j], axis=1) == codes_b
                product = jnp.where(same, product, 0.0).reshape(TILES, 16, 256)
                acc[pl.ds(j * 16, 16), :] += jnp.sum(product, axis=0)

    low_lanes = lax.broadcasted_iota(jnp.int32, (32, LANES), 1) < 64
    for panel in range(4):
        product = acc[pl.ds(panel * 64, 64), :]
        norms = row_norms[pl.ds(panel * 4, 4)].reshape(64, LANES)
        norms = jnp.concatenate([norms, norms], axis=1)
        ratio = product / (norms + norms_across - product)
        ratio = jnp.where(panel < x, pltpu.roll(ratio, 240, 1), ratio)
        for half in range(2):
            first = ratio[0:32, half * 128 : half * 128 + 128]
            second = ratio[32:64, half * 128 : half * 128 + 128]
            out[0, panel, half] = jnp.where(low_lanes, first, pltpu.roll(second, 64, 1))
            out[1, panel, half] = jnp.where(low_lanes, pltpu.roll(first, 64, 1), second)


def place_kernel(arrived, out, tall):
    x = lax.axis_index("x")
    take = lax.broadcasted_iota(jnp.int32, (256, 512), 0)
    give = lax.broadcasted_iota(jnp.int32, (256, 512), 1)
    base = ((take >> 4) & 7) * 64 + (take & 15) * 4 + (take >> 7)
    results = []
    for delta in range(4):
        xs = (x - delta) & 3
        total = jnp.zeros((32, 512), F32)
        for yh in range(2):
            shift = (base + 2 * yh == give).astype(BF16)
            block = jnp.concatenate([arrived[0, xs, yh], arrived[1, xs, yh]], axis=1)
            high = block.astype(BF16)
            rest = block - high.astype(F32)
            middle = rest.astype(BF16)
            low = (rest - middle.astype(F32)).astype(BF16)
            stacked = jnp.concatenate([high, middle, low], axis=0)
            moved = jnp.dot(stacked, shift, preferred_element_type=F32)
            total = total + ((moved[0:32] + moved[32:64]) + moved[64:96])
        results.append(total)
    low_lanes = lax.broadcasted_iota(jnp.int32, (32, LANES), 1) < 64
    for h in range(2):
        for pair in range(2):
            for t in range(4):
                place = h * 256 + (t // 2) * 128
                even = results[2 * pair][:, place : place + 128]
                odd = results[2 * pair + 1][:, place : place + 128]
                if t % 2 == 0:
                    block = jnp.where(low_lanes, even, pltpu.roll(odd, 64, 1))
                else:
                    block = jnp.where(low_lanes, pltpu.roll(even, 64, 1), odd)
                for s in range(2):
                    tall[2 * t + pair, pl.ds(2 * h + s, 16, stride=4), :] = block[s * 16 : s * 16 + 16]
    for group in range(8):
        out[:, group * 128 : group * 128 + 128] = tall[group]


def step(block, axis, distance):
    size = lax.axis_size(axis)
    return lax.ppermute(block, axis, [((i - distance) % size, i) for i in range(size)])


def on_device(tile_values, tile_ids, doc_tiles, row_counts):
    c = lax.axis_index("c")
    sending, source = pl.pallas_call(
        pack_kernel,
        out_shape=(
            jax.ShapeDtypeStruct((64, SENT, LANES), BF16),
            jax.ShapeDtypeStruct((16,), jnp.int32),
        ),
        in_specs=[SMEM, SMEM, VMEM, VMEM],
        out_specs=(VMEM, SMEM),
        scratch_shapes=[pltpu.VMEM((128, LANES), F32)],
        compiler_params=params(16),
    )(row_counts, doc_tiles, tile_ids, tile_values)
    arrived = lax.all_to_all(sending, ("z", "yl", "x"), 0, 0, tiled=True)
    piece, spread = pl.pallas_call(
        arrange_kernel,
        out_shape=(
            jax.ShapeDtypeStruct((PIECE, 16, LANES), BF16),
            jax.ShapeDtypeStruct((16, PIECE, 16, LANES), BF16),
        ),
        in_specs=[SMEM, VMEM],
        out_specs=(VMEM, VMEM),
        scratch_shapes=[pltpu.VMEM((16 * SENT, LANES), F32)],
        compiler_params=params(16),
    )(source, arrived)
    rows = lax.all_to_all(spread, ("x", "yh", "yl"), 0, 0, tiled=True)
    ring = [piece] + [None] * 7
    behind, ahead = piece, piece
    for distance in range(1, 4):
        behind, ahead = step(behind, "z", 1), step(ahead, "z", -1)
        ring[distance], ring[8 - distance] = behind, ahead
    ring[4] = step(behind, "z", 1)
    own = jnp.stack(ring)
    other = step(own, "c", 1)
    blocks = pl.pallas_call(
        compare_kernel,
        out_shape=jax.ShapeDtypeStruct((2, 4, 2, 32, LANES), F32),
        in_specs=[VMEM, VMEM, VMEM],
        out_specs=VMEM,
        scratch_shapes=[
            pltpu.VMEM((TILES, 256, LANES), BF16),
            pltpu.VMEM((256, LANES), F32),
            pltpu.VMEM((16, TILES, 16, LANES), F32),
            pltpu.VMEM((16, 16, LANES), F32),
            pltpu.VMEM((256, 256), F32),
        ],
        compiler_params=params(40),
    )(rows, own, other)
    swapped = step(blocks[1 - c], "c", 1)
    kept = blocks[c]
    results = jnp.where(c == 0, jnp.stack([kept, swapped]), jnp.stack([swapped, kept]))
    results = lax.all_to_all(
        results.reshape(16, 32, LANES), ("yl", "x", "yh"), 0, 0, tiled=True
    ).reshape(2, 4, 2, 32, LANES)
    return pl.pallas_call(
        place_kernel,
        out_shape=jax.ShapeDtypeStruct((64, 1024), F32),
        in_specs=[VMEM],
        out_specs=VMEM,
        scratch_shapes=[pltpu.VMEM((8, 64, LANES), F32)],
        compiler_params=params(16),
    )(results)


def solution(mesh):
    fine = Mesh(mesh.devices.reshape(8, 2, 4, 2, 2), ("z", "yl", "x", "yh", "c"))
    rows, columns = ("z", "yl", "x"), ("yh", "c")
    placed = (P(rows, None, None), P(rows, None), P(rows), P())
    return jax.shard_map(
        on_device, mesh=fine, in_specs=placed, out_specs=P(rows, columns), check_vma=False
    )
```

```python
import jax
import jax.numpy as jnp
from jax import lax
from jax.experimental import pallas as pl
from jax.experimental.pallas import tpu as pltpu
from jax.sharding import Mesh
from jax.sharding import PartitionSpec as P

TILES = 16
LANES = 128
SENT = 18
PIECE = TILES + 1
BF16 = jnp.bfloat16
F32 = jnp.float32
VMEM = pl.BlockSpec(memory_space=pltpu.VMEM)
ANY = pl.BlockSpec(memory_space=pl.ANY)
SMEM = pl.BlockSpec(memory_space=pltpu.SMEM)


def params(mib):
    return pltpu.CompilerParams(vmem_limit_bytes=mib * 2**20)


def source_kernel(counts, source):
    z, yl, x = lax.axis_index("z"), lax.axis_index("yl"), lax.axis_index("x")
    yh, c = lax.axis_index("yh"), lax.axis_index("c")
    base = (yh * 2 + yl) * 64 + z * 8 + c * 4 + x

    def scan(e, begin):
        end = begin + counts[e]
        number = begin + ((base - begin) & 255)

        @pl.when(number < end)
        def _():
            source[number >> 8] = e

        return end

    lax.fori_loop(0, 64, scan, jnp.int32(0), unroll=8)


def pack_kernel(counts_in, tiles_in, ids_in, values_in, out, counts, tiles, ids, values, wide_ids, sems):
    moves = [
        pltpu.make_async_copy(counts_in, counts, sems.at[0]),
        pltpu.make_async_copy(ids_in, ids, sems.at[1]),
        pltpu.make_async_copy(tiles_in, tiles, sems.at[2]),
        pltpu.make_async_copy(values_in, values, sems.at[3]),
    ]
    for move in moves:
        move.start()
    yh, c = lax.axis_index("yh"), lax.axis_index("c")
    here = lax.axis_index("z") * 8 + lax.axis_index("yl") * 4 + lax.axis_index("x")
    moves[0].wait()
    own_begin = lax.fori_loop(
        0, 64, lambda e, begin: begin + jnp.where(e < here, counts[e], 0), jnp.int32(0), unroll=16
    )
    moves[1].wait()
    tall_ids = jnp.concatenate([ids[...].astype(F32), jnp.zeros((LANES - TILES, LANES), F32)], axis=0)
    wide_ids[...] = jnp.transpose(tall_ids, (1, 0))
    moves[2].wait()
    moves[3].wait()
    tile_line = lax.broadcasted_iota(jnp.int32, (TILES, LANES), 0)

    def fill(t, carry):
        wanted = (yh * 2 + ((t >> 2) & 1)) * 64 + (t >> 3) * 8 + c * 4 + (t & 3)
        slot = jnp.minimum((wanted - own_begin) & 255, 127)
        document = jnp.where(tile_line < tiles[slot], values[slot].astype(F32), 0.0)
        codes = jnp.broadcast_to(wide_ids[pl.ds(slot, 1), :], (SENT - TILES, LANES))
        whole = jnp.concatenate([document, codes], axis=0).astype(BF16)
        out[t] = whole.reshape(SENT // 2, 2, LANES)
        return carry

    lax.fori_loop(0, 64, fill, 0, unroll=8)


def arrange_kernel(source, arrived, piece, spread, lines):
    for m in range(16):
        lines[pl.ds(m * SENT, SENT), :] = arrived[source[m]].reshape(SENT, LANES).astype(F32)
    total = jnp.zeros((16, LANES), F32)
    parts = []
    for k in range(TILES):
        part = lines[pl.ds(k, 16, stride=SENT), :]
        total = total + part * part
        parts.append(part.astype(BF16))
    norms = jnp.sum(total, axis=1, keepdims=True)
    high = norms.astype(BF16).astype(F32)
    middle = (norms - high).astype(BF16).astype(F32)
    low = norms - high - middle
    lane = lax.broadcasted_iota(jnp.int32, (16, LANES), 1)
    codes = lines[pl.ds(TILES, 16, stride=SENT), :]
    codes = jnp.where(lane == 16, high, codes)
    codes = jnp.where(lane == 17, middle, codes)
    codes = jnp.where(lane == 18, low, codes)
    parts.append(codes.astype(BF16))
    whole = jnp.concatenate([part[None] for part in parts], axis=0)
    piece[...] = whole
    for j in range(16):
        spread[j] = whole


def compare(rows, pieces, row_codes, piece_codes, acc):
    for j in range(16):
        row_codes[j * 16 : j * 16 + 16, :] = rows[j, TILES].astype(F32)
    across = jnp.transpose(row_codes[...], (1, 0))
    row_codes[0:128, :] = across[:, 0:128]
    row_codes[128:256, :] = across[:, 128:256]
    piece_norms = []
    for d in range(8):
        codes = pieces[d, TILES].astype(F32)
        for k in range(TILES):
            piece_codes[d, k] = jnp.broadcast_to(codes[:, k : k + 1], (16, LANES))
        norms = codes[:, 16:17] + codes[:, 17:18] + codes[:, 18:19]
        piece_norms.append(jnp.broadcast_to(norms, (16, 256)))
    acc[...] = jnp.zeros_like(acc)

    for k in range(TILES):
        weights = jnp.transpose(rows[:, k].reshape(256, LANES), (1, 0))
        codes_k = jnp.concatenate(
            [row_codes[pl.ds(k, 1), :], row_codes[pl.ds(128 + k, 1), :]], axis=1
        )
        for d in range(8):
            left = pieces[d, 0:TILES].reshape(256, LANES)
            product = jnp.dot(left, weights, preferred_element_type=F32)
            codes_d = piece_codes[d].reshape(256, LANES)
            same = jnp.concatenate([codes_d, codes_d], axis=1) == codes_k
            product = jnp.where(same, product, 0.0).reshape(TILES, 16, 256)
            acc[d] += jnp.sum(product, axis=0)

    norms_across = across[16:17] + across[17:18] + across[18:19]
    for d in range(8):
        acc[d] = acc[d] / (piece_norms[d] + norms_across - acc[d])


def own_kernel(rows, own, out, row_codes, piece_codes):
    compare(rows, own, row_codes, piece_codes, out)


def other_kernel(rows, other, own_ratio, out, row_codes, piece_codes, acc, tall):
    x, c = lax.axis_index("x"), lax.axis_index("c")
    compare(rows, other, row_codes, piece_codes, acc)
    for u in range(16):
        tall[u * 16 : u * 16 + 16, :] = own_ratio[u // 2] if u % 2 == 0 else acc[((u + 1) // 2 - c) & 7]
    low_lanes = lax.broadcasted_iota(jnp.int32, (32, LANES), 1) < 64
    for panel in range(4):
        if panel % 2 == 0:
            wide = jnp.transpose(tall[:, panel * 64 : panel * 64 + 128], (1, 0))
        ratio = wide[(panel % 2) * 64 : (panel % 2) * 64 + 64]
        ratio = jnp.where(panel < x, pltpu.roll(ratio, 240, 1), ratio)
        for half in range(2):
            first = ratio[0:32, half * 128 : half * 128 + 128]
            second = ratio[32:64, half * 128 : half * 128 + 128]
            out[0, panel, half] = jnp.where(low_lanes, first, pltpu.roll(second, 64, 1))
            out[1, panel, half] = jnp.where(low_lanes, pltpu.roll(first, 64, 1), second)


def place_kernel(arrived, out, tall):
    x = lax.axis_index("x")
    take = lax.broadcasted_iota(jnp.int32, (256, 512), 0)
    give = lax.broadcasted_iota(jnp.int32, (256, 512), 1)
    base = ((take >> 4) & 7) * 64 + (take & 15) * 4 + (take >> 7)
    results = []
    for delta in range(4):
        xs = (x - delta) & 3
        total = jnp.zeros((32, 512), F32)
        for yh in range(2):
            shift = (base + 2 * yh == give).astype(BF16)
            block = jnp.concatenate([arrived[0, xs, yh], arrived[1, xs, yh]], axis=1)
            high = block.astype(BF16)
            rest = block - high.astype(F32)
            middle = rest.astype(BF16)
            low = (rest - middle.astype(F32)).astype(BF16)
            stacked = jnp.concatenate([high, middle, low], axis=0)
            moved = jnp.dot(stacked, shift, preferred_element_type=F32)
            total = total + ((moved[0:32] + moved[32:64]) + moved[64:96])
        results.append(total)
    low_lanes = lax.broadcasted_iota(jnp.int32, (32, LANES), 1) < 64
    for h in range(2):
        for pair in range(2):
            for t in range(4):
                place = h * 256 + (t // 2) * 128
                even = results[2 * pair][:, place : place + 128]
                odd = results[2 * pair + 1][:, place : place + 128]
                if t % 2 == 0:
                    block = jnp.where(low_lanes, even, pltpu.roll(odd, 64, 1))
                else:
                    block = jnp.where(low_lanes, pltpu.roll(even, 64, 1), odd)
                for s in range(2):
                    tall[2 * t + pair, pl.ds(2 * h + s, 16, stride=4), :] = block[s * 16 : s * 16 + 16]
    for group in range(8):
        out[:, group * 128 : group * 128 + 128] = tall[group]


def step(block, axis, distance):
    size = lax.axis_size(axis)
    return lax.ppermute(block, axis, [((i - distance) % size, i) for i in range(size)])


def on_device(tile_values, tile_ids, doc_tiles, row_counts):
    c = lax.axis_index("c")
    sending = pl.pallas_call(
        pack_kernel,
        out_shape=jax.ShapeDtypeStruct((64, SENT // 2, 2, LANES), BF16),
        in_specs=[ANY, ANY, ANY, ANY],
        out_specs=VMEM,
        scratch_shapes=[
            pltpu.SMEM((64,), jnp.int32),
            pltpu.SMEM((128,), jnp.int32),
            pltpu.VMEM((TILES, LANES), jnp.int32),
            pltpu.VMEM((128, TILES, LANES), BF16),
            pltpu.VMEM((128, LANES), F32),
            pltpu.SemaphoreType.DMA((4,)),
        ],
        compiler_params=params(60),
    )(row_counts, doc_tiles, tile_ids.T, tile_values)
    source = pl.pallas_call(
        source_kernel,
        out_shape=jax.ShapeDtypeStruct((16,), jnp.int32),
        in_specs=[SMEM],
        out_specs=SMEM,
        compiler_params=params(4),
        cost_estimate=pl.CostEstimate(flops=2**30, bytes_accessed=2**20, transcendentals=0),
    )(row_counts)
    arrived = lax.all_to_all(sending, ("z", "yl", "x"), 0, 0, tiled=True)
    piece, spread = pl.pallas_call(
        arrange_kernel,
        out_shape=(
            jax.ShapeDtypeStruct((PIECE, 16, LANES), BF16),
            jax.ShapeDtypeStruct((16, PIECE, 16, LANES), BF16),
        ),
        in_specs=[SMEM, VMEM],
        out_specs=(VMEM, VMEM),
        scratch_shapes=[pltpu.VMEM((16 * SENT, LANES), F32)],
        compiler_params=params(16),
    )(source, arrived)
    rows = lax.all_to_all(spread, ("x", "yh", "yl"), 0, 0, tiled=True)
    ring = [piece] + [None] * 7
    ring[1] = step(piece, "z", 1)
    ahead, behind = lax.optimization_barrier((piece, ring[1]))
    for distance in range(1, 4):
        behind, ahead = step(behind, "z", 1), step(ahead, "z", -1)
        ring[distance + 1], ring[8 - distance] = behind, ahead
    own = jnp.stack(ring)
    other = step(own, "c", 1)
    codes_scratch = [pltpu.VMEM((256, LANES), F32), pltpu.VMEM((8, TILES, 16, LANES), F32)]
    cost = pl.CostEstimate(flops=2 * 4096 * 2048 * LANES, bytes_accessed=2**21, transcendentals=0)
    own_ratio = pl.pallas_call(
        own_kernel,
        out_shape=jax.ShapeDtypeStruct((8, 16, 256), F32),
        in_specs=[VMEM, VMEM],
        out_specs=VMEM,
        scratch_shapes=codes_scratch,
        compiler_params=params(32),
        cost_estimate=cost,
    )(rows, own)
    blocks = pl.pallas_call(
        other_kernel,
        out_shape=jax.ShapeDtypeStruct((2, 4, 2, 32, LANES), F32),
        in_specs=[VMEM, VMEM, VMEM],
        out_specs=VMEM,
        scratch_shapes=codes_scratch + [pltpu.VMEM((8, 16, 256), F32), pltpu.VMEM((256, 256), F32)],
        compiler_params=params(32),
        cost_estimate=cost,
    )(rows, other, own_ratio)
    swapped = step(blocks[1 - c], "c", 1)
    kept = blocks[c]
    results = jnp.where(c == 0, jnp.stack([kept, swapped]), jnp.stack([swapped, kept]))
    results = lax.all_to_all(
        results.reshape(16, 32, LANES), ("yl", "x", "yh"), 0, 0, tiled=True
    ).reshape(2, 4, 2, 32, LANES)
    return pl.pallas_call(
        place_kernel,
        out_shape=jax.ShapeDtypeStruct((64, 1024), F32),
        in_specs=[VMEM],
        out_specs=VMEM,
        scratch_shapes=[pltpu.VMEM((8, 64, LANES), F32)],
        compiler_params=params(16),
    )(results)


def solution(mesh):
    fine = Mesh(mesh.devices.reshape(8, 2, 4, 2, 2), ("z", "yl", "x", "yh", "c"))
    rows, columns = ("z", "yl", "x"), ("yh", "c")
    placed = (P(rows, None, None), P(rows, None), P(rows), P())
    return jax.shard_map(
        on_device, mesh=fine, in_specs=placed, out_specs=P(rows, columns), check_vma=False
    )
```

```python
import functools

import jax
import jax.numpy as jnp
from jax import lax
from jax.experimental import pallas as pl
from jax.experimental.pallas import tpu as pltpu
from jax.sharding import Mesh
from jax.sharding import PartitionSpec as P

TILES = 16
LANES = 128
SENT = 18
PIECE = TILES + 1
BF16 = jnp.bfloat16
F32 = jnp.float32
VMEM = pl.BlockSpec(memory_space=pltpu.VMEM)
ANY = pl.BlockSpec(memory_space=pl.ANY)
SMEM = pl.BlockSpec(memory_space=pltpu.SMEM)


def cost(pieces):
    return pl.CostEstimate(flops=2 * 4096 * 256 * pieces * LANES, bytes_accessed=2**21, transcendentals=0)


def params(mib):
    return pltpu.CompilerParams(vmem_limit_bytes=mib * 2**20)


def source_kernel(counts, source):
    z, yl, x = lax.axis_index("z"), lax.axis_index("yl"), lax.axis_index("x")
    yh, c = lax.axis_index("yh"), lax.axis_index("c")
    base = (yh * 2 + yl) * 64 + z * 8 + c * 4 + x

    def scan(e, begin):
        end = begin + counts[e]
        number = begin + ((base - begin) & 255)

        @pl.when(number < end)
        def _():
            source[number >> 8] = e

        return end

    lax.fori_loop(0, 64, scan, jnp.int32(0), unroll=8)


def pack_kernel(counts_in, tiles_in, ids_in, values_in, out, counts, tiles, ids, values, wide_ids, sems):
    moves = [
        pltpu.make_async_copy(counts_in, counts, sems.at[0]),
        pltpu.make_async_copy(ids_in, ids, sems.at[1]),
        pltpu.make_async_copy(tiles_in, tiles, sems.at[2]),
        pltpu.make_async_copy(values_in, values, sems.at[3]),
    ]
    for move in moves:
        move.start()
    yh, c = lax.axis_index("yh"), lax.axis_index("c")
    here = lax.axis_index("z") * 8 + lax.axis_index("yl") * 4 + lax.axis_index("x")
    moves[0].wait()
    own_begin = lax.fori_loop(
        0, 64, lambda e, begin: begin + jnp.where(e < here, counts[e], 0), jnp.int32(0), unroll=16
    )
    moves[1].wait()
    tall_ids = jnp.concatenate([ids[...].astype(F32), jnp.zeros((LANES - TILES, LANES), F32)], axis=0)
    wide_ids[...] = jnp.transpose(tall_ids, (1, 0))
    moves[2].wait()
    moves[3].wait()
    tile_line = lax.broadcasted_iota(jnp.int32, (TILES, LANES), 0)

    def fill(t, carry):
        wanted = (yh * 2 + ((t >> 2) & 1)) * 64 + (t >> 3) * 8 + c * 4 + (t & 3)
        slot = jnp.minimum((wanted - own_begin) & 255, 127)
        document = jnp.where(tile_line < tiles[slot], values[slot].astype(F32), 0.0)
        codes = jnp.broadcast_to(wide_ids[pl.ds(slot, 1), :], (SENT - TILES, LANES))
        whole = jnp.concatenate([document, codes], axis=0).astype(BF16)
        out[t] = whole.reshape(SENT // 2, 2, LANES)
        return carry

    lax.fori_loop(0, 64, fill, 0, unroll=8)


def arrange_kernel(source, arrived, piece, spread, lines):
    for m in range(16):
        lines[pl.ds(m * SENT, SENT), :] = arrived[source[m]].reshape(SENT, LANES).astype(F32)
    total = jnp.zeros((16, LANES), F32)
    parts = []
    for k in range(TILES):
        part = lines[pl.ds(k, 16, stride=SENT), :]
        total = total + part * part
        parts.append(part.astype(BF16))
    norms = jnp.sum(total, axis=1, keepdims=True)
    high = norms.astype(BF16).astype(F32)
    middle = (norms - high).astype(BF16).astype(F32)
    low = norms - high - middle
    lane = lax.broadcasted_iota(jnp.int32, (16, LANES), 1)
    codes = lines[pl.ds(TILES, 16, stride=SENT), :]
    codes = jnp.where(lane == 16, high, codes)
    codes = jnp.where(lane == 17, middle, codes)
    codes = jnp.where(lane == 18, low, codes)
    parts.append(codes.astype(BF16))
    whole = jnp.concatenate([part[None] for part in parts], axis=0)
    piece[...] = whole
    for j in range(16):
        spread[j] = whole


def compare(rows, pieces, chosen, row_codes, piece_codes, acc):
    for j in range(16):
        row_codes[j * 16 : j * 16 + 16, :] = rows[j, TILES].astype(F32)
    across = jnp.transpose(row_codes[...], (1, 0))
    row_codes[0:128, :] = across[:, 0:128]
    row_codes[128:256, :] = across[:, 128:256]
    piece_norms = []
    for d, place in enumerate(chosen):
        codes = pieces[place, TILES].astype(F32)
        for k in range(TILES):
            piece_codes[d, k] = jnp.broadcast_to(codes[:, k : k + 1], (16, LANES))
        norms = codes[:, 16:17] + codes[:, 17:18] + codes[:, 18:19]
        piece_norms.append(jnp.broadcast_to(norms, (16, 256)))
    acc[...] = jnp.zeros_like(acc)
    for k in range(TILES):
        weights = jnp.transpose(rows[:, k].reshape(256, LANES), (1, 0))
        codes_k = jnp.concatenate(
            [row_codes[pl.ds(k, 1), :], row_codes[pl.ds(128 + k, 1), :]], axis=1
        )
        for d, place in enumerate(chosen):
            left = pieces[place, 0:TILES].reshape(256, LANES)
            product = jnp.dot(left, weights, preferred_element_type=F32)
            codes_d = piece_codes[d].reshape(256, LANES)
            same = jnp.concatenate([codes_d, codes_d], axis=1) == codes_k
            product = jnp.where(same, product, 0.0).reshape(TILES, 16, 256)
            acc[d] += jnp.sum(product, axis=0)
    norms_across = across[16:17] + across[17:18] + across[18:19]
    for d in range(len(chosen)):
        acc[d] = acc[d] / (piece_norms[d] + norms_across - acc[d])


def own_kernel(rows, own, out, row_codes, piece_codes):
    compare(rows, own, list(range(8)), row_codes, piece_codes, out)


def other_kernel(kept, rows, other, own_ratio, out, row_codes, piece_codes, acc, tall):
    x, c = lax.axis_index("x"), lax.axis_index("c")
    core = c if kept else 1 - c
    odd = [4 * core + 1, 4 * core + 3, 4 * core + 9, 4 * core + 11]
    chosen = [(((u + 1) >> 1) - c) & 7 for u in odd]
    compare(rows, other, chosen, row_codes, piece_codes, acc)
    low_lanes = lax.broadcasted_iota(jnp.int32, (32, LANES), 1) < 64
    for half in range(2):
        for i in range(5):
            if i % 2 == 0:
                part = own_ratio[(4 * half + 2 * core + i // 2) & 7]
            else:
                part = acc[2 * half + i // 2]
            tall[half, i * 16 : i * 16 + 16, :] = part
        wide = jnp.transpose(tall[half], (1, 0))
        for panel in range(4):
            ratio = wide[panel * 64 : panel * 64 + 64]
            ratio = jnp.where(panel < x, pltpu.roll(ratio, 112, 1), ratio)
            out[panel, half] = jnp.where(low_lanes, ratio[0:32], pltpu.roll(ratio[32:64], 64, 1))


def place_kernel(arrived, out, tall):
    x = lax.axis_index("x")
    take = lax.broadcasted_iota(jnp.int32, (256, 512), 0)
    give = lax.broadcasted_iota(jnp.int32, (256, 512), 1)
    base = ((take >> 4) & 7) * 64 + (take & 15) * 4 + (take >> 7)
    results = []
    for delta in range(4):
        xs = (x - delta) & 3
        total = jnp.zeros((32, 512), F32)
        for yh in range(2):
            shift = (base + 2 * yh == give).astype(BF16)
            block = jnp.concatenate([arrived[0, xs, yh], arrived[1, xs, yh]], axis=1)
            high = block.astype(BF16)
            rest = block - high.astype(F32)
            middle = rest.astype(BF16)
            low = (rest - middle.astype(F32)).astype(BF16)
            stacked = jnp.concatenate([high, middle, low], axis=0)
            moved = jnp.dot(stacked, shift, preferred_element_type=F32)
            total = total + ((moved[0:32] + moved[32:64]) + moved[64:96])
        results.append(total)
    low_lanes = lax.broadcasted_iota(jnp.int32, (32, LANES), 1) < 64
    for h in range(2):
        for pair in range(2):
            for t in range(4):
                place = h * 256 + (t // 2) * 128
                even = results[2 * pair][:, place : place + 128]
                odd = results[2 * pair + 1][:, place : place + 128]
                if t % 2 == 0:
                    block = jnp.where(low_lanes, even, pltpu.roll(odd, 64, 1))
                else:
                    block = jnp.where(low_lanes, pltpu.roll(even, 64, 1), odd)
                for s in range(2):
                    tall[2 * t + pair, pl.ds(2 * h + s, 16, stride=4), :] = block[s * 16 : s * 16 + 16]
    for group in range(8):
        out[:, group * 128 : group * 128 + 128] = tall[group]


def step(block, axis, distance):
    size = lax.axis_size(axis)
    return lax.ppermute(block, axis, [((i - distance) % size, i) for i in range(size)])


def on_device(tile_values, tile_ids, doc_tiles, row_counts):
    c = lax.axis_index("c")
    sending = pl.pallas_call(
        pack_kernel,
        out_shape=jax.ShapeDtypeStruct((64, SENT // 2, 2, LANES), BF16),
        in_specs=[ANY, ANY, ANY, ANY],
        out_specs=VMEM,
        scratch_shapes=[
            pltpu.SMEM((64,), jnp.int32),
            pltpu.SMEM((128,), jnp.int32),
            pltpu.VMEM((TILES, LANES), jnp.int32),
            pltpu.VMEM((128, TILES, LANES), BF16),
            pltpu.VMEM((128, LANES), F32),
            pltpu.SemaphoreType.DMA((4,)),
        ],
        compiler_params=params(60),
    )(row_counts, doc_tiles, tile_ids.T, tile_values)
    source = pl.pallas_call(
        source_kernel,
        out_shape=jax.ShapeDtypeStruct((16,), jnp.int32),
        in_specs=[SMEM],
        out_specs=SMEM,
        compiler_params=params(4),
        cost_estimate=pl.CostEstimate(flops=2**30, bytes_accessed=2**20, transcendentals=0),
    )(row_counts)
    arrived = lax.all_to_all(sending, ("z", "yl", "x"), 0, 0, tiled=True)
    piece, spread = pl.pallas_call(
        arrange_kernel,
        out_shape=(
            jax.ShapeDtypeStruct((PIECE, 16, LANES), BF16),
            jax.ShapeDtypeStruct((16, PIECE, 16, LANES), BF16),
        ),
        in_specs=[SMEM, VMEM],
        out_specs=(VMEM, VMEM),
        scratch_shapes=[pltpu.VMEM((16 * SENT, LANES), F32)],
        compiler_params=params(16),
    )(source, arrived)
    rows = lax.all_to_all(spread, ("x", "yh", "yl"), 0, 0, tiled=True)
    ring = [piece] + [None] * 7
    ring[1] = step(piece, "z", 1)
    ahead, behind = lax.optimization_barrier((piece, ring[1]))
    for distance in range(1, 4):
        behind, ahead = step(behind, "z", 1), step(ahead, "z", -1)
        ring[distance + 1], ring[8 - distance] = behind, ahead
    own = jnp.stack(ring)
    other = step(own, "c", 1)
    own_ratio = pl.pallas_call(
        own_kernel,
        out_shape=jax.ShapeDtypeStruct((8, 16, 256), F32),
        in_specs=[VMEM, VMEM],
        out_specs=VMEM,
        scratch_shapes=[pltpu.VMEM((256, LANES), F32), pltpu.VMEM((8, TILES, 16, LANES), F32)],
        compiler_params=params(32),
        cost_estimate=cost(8),
    )(rows, own)

    def finish(kept):
        return pl.pallas_call(
            functools.partial(other_kernel, kept),
            out_shape=jax.ShapeDtypeStruct((4, 2, 32, LANES), F32),
            in_specs=[VMEM, VMEM, VMEM],
            out_specs=VMEM,
            scratch_shapes=[
                pltpu.VMEM((256, LANES), F32),
                pltpu.VMEM((4, TILES, 16, LANES), F32),
                pltpu.VMEM((4, 16, 256), F32),
                pltpu.VMEM((2, LANES, 256), F32),
            ],
            compiler_params=params(32),
            cost_estimate=cost(4),
        )(rows, other, own_ratio)

    swapped = step(finish(False), "c", 1)
    kept = finish(True)
    results = jnp.where(c == 0, jnp.stack([kept, swapped]), jnp.stack([swapped, kept]))
    results = lax.all_to_all(
        results.reshape(16, 32, LANES), ("yl", "x", "yh"), 0, 0, tiled=True
    ).reshape(2, 4, 2, 32, LANES)
    return pl.pallas_call(
        place_kernel,
        out_shape=jax.ShapeDtypeStruct((64, 1024), F32),
        in_specs=[VMEM],
        out_specs=VMEM,
        scratch_shapes=[pltpu.VMEM((8, 64, LANES), F32)],
        compiler_params=params(16),
    )(results)


def solution(mesh):
    fine = Mesh(mesh.devices.reshape(8, 2, 4, 2, 2), ("z", "yl", "x", "yh", "c"))
    rows, columns = ("z", "yl", "x"), ("yh", "c")
    placed = (P(rows, None, None), P(rows, None), P(rows), P())
    return jax.shard_map(
        on_device, mesh=fine, in_specs=placed, out_specs=P(rows, columns), check_vma=False
    )
```

```python
import functools

import jax
import jax.numpy as jnp
from jax import lax
from jax.experimental import pallas as pl
from jax.experimental.pallas import tpu as pltpu
from jax.sharding import Mesh
from jax.sharding import PartitionSpec as P

TILES = 16
LANES = 128
SENT = 18
PIECE = TILES + 1
EARLY, LATE = (0, 1, 2, 3, 6, 7), (4, 5)
BF16 = jnp.bfloat16
F32 = jnp.float32
VMEM = pl.BlockSpec(memory_space=pltpu.VMEM)
ANY = pl.BlockSpec(memory_space=pl.ANY)
SMEM = pl.BlockSpec(memory_space=pltpu.SMEM)


def cost(pieces):
    return pl.CostEstimate(flops=2 * 4096 * 256 * pieces * LANES, bytes_accessed=2**21, transcendentals=0)


def params(mib):
    return pltpu.CompilerParams(vmem_limit_bytes=mib * 2**20)


def source_kernel(counts, source):
    z, yl, x = lax.axis_index("z"), lax.axis_index("yl"), lax.axis_index("x")
    yh, c = lax.axis_index("yh"), lax.axis_index("c")
    base = (yh * 2 + yl) * 64 + z * 8 + c * 4 + x

    def scan(e, begin):
        end = begin + counts[e]
        number = begin + ((base - begin) & 255)

        @pl.when(number < end)
        def _():
            source[number >> 8] = e

        return end

    lax.fori_loop(0, 64, scan, jnp.int32(0), unroll=8)


def pack_kernel(counts_in, tiles_in, ids_in, values_in, out, counts, tiles, ids, values, wide_ids, sems):
    moves = [
        pltpu.make_async_copy(counts_in, counts, sems.at[0]),
        pltpu.make_async_copy(ids_in, ids, sems.at[1]),
        pltpu.make_async_copy(tiles_in, tiles, sems.at[2]),
        pltpu.make_async_copy(values_in, values, sems.at[3]),
    ]
    for move in moves:
        move.start()
    yh, c = lax.axis_index("yh"), lax.axis_index("c")
    here = lax.axis_index("z") * 8 + lax.axis_index("yl") * 4 + lax.axis_index("x")
    moves[0].wait()
    own_begin = lax.fori_loop(
        0, 64, lambda e, begin: begin + jnp.where(e < here, counts[e], 0), jnp.int32(0), unroll=16
    )
    moves[1].wait()
    tall_ids = jnp.concatenate([ids[...].astype(F32), jnp.zeros((LANES - TILES, LANES), F32)], axis=0)
    wide_ids[...] = jnp.transpose(tall_ids, (1, 0))
    moves[2].wait()
    moves[3].wait()
    tile_line = lax.broadcasted_iota(jnp.int32, (TILES, LANES), 0)

    def fill(t, carry):
        wanted = (yh * 2 + ((t >> 2) & 1)) * 64 + (t >> 3) * 8 + c * 4 + (t & 3)
        slot = jnp.minimum((wanted - own_begin) & 255, 127)
        document = jnp.where(tile_line < tiles[slot], values[slot].astype(F32), 0.0)
        codes = jnp.broadcast_to(wide_ids[pl.ds(slot, 1), :], (SENT - TILES, LANES))
        whole = jnp.concatenate([document, codes], axis=0).astype(BF16)
        out[t] = whole.reshape(SENT // 2, 2, LANES)
        return carry

    lax.fori_loop(0, 64, fill, 0, unroll=8)


def arrange_kernel(source, arrived, piece, spread, lines):
    for m in range(16):
        lines[pl.ds(m * SENT, SENT), :] = arrived[source[m]].reshape(SENT, LANES).astype(F32)
    total = jnp.zeros((16, LANES), F32)
    parts = []
    for k in range(TILES):
        part = lines[pl.ds(k, 16, stride=SENT), :]
        total = total + part * part
        parts.append(part.astype(BF16))
    norms = jnp.sum(total, axis=1, keepdims=True)
    high = norms.astype(BF16).astype(F32)
    middle = (norms - high).astype(BF16).astype(F32)
    low = norms - high - middle
    lane = lax.broadcasted_iota(jnp.int32, (16, LANES), 1)
    codes = lines[pl.ds(TILES, 16, stride=SENT), :]
    codes = jnp.where(lane == 16, high, codes)
    codes = jnp.where(lane == 17, middle, codes)
    codes = jnp.where(lane == 18, low, codes)
    parts.append(codes.astype(BF16))
    whole = jnp.concatenate([part[None] for part in parts], axis=0)
    piece[...] = whole
    for j in range(16):
        spread[j] = whole


def compare(rows, pieces, chosen, row_codes, piece_codes, acc):
    for j in range(16):
        row_codes[j * 16 : j * 16 + 16, :] = rows[j, TILES].astype(F32)
    across = jnp.transpose(row_codes[...], (1, 0))
    row_codes[0:128, :] = across[:, 0:128]
    row_codes[128:256, :] = across[:, 128:256]
    piece_norms = []
    for d, place in enumerate(chosen):
        codes = pieces[place, TILES].astype(F32)
        for k in range(TILES):
            piece_codes[d, k] = jnp.broadcast_to(codes[:, k : k + 1], (16, LANES))
        norms = codes[:, 16:17] + codes[:, 17:18] + codes[:, 18:19]
        piece_norms.append(jnp.broadcast_to(norms, (16, 256)))
    acc[...] = jnp.zeros_like(acc)
    for k in range(TILES):
        weights = jnp.transpose(rows[:, k].reshape(256, LANES), (1, 0))
        codes_k = jnp.concatenate(
            [row_codes[pl.ds(k, 1), :], row_codes[pl.ds(128 + k, 1), :]], axis=1
        )
        for d, place in enumerate(chosen):
            left = pieces[place, 0:TILES].reshape(256, LANES)
            product = jnp.dot(left, weights, preferred_element_type=F32)
            codes_d = piece_codes[d].reshape(256, LANES)
            same = jnp.concatenate([codes_d, codes_d], axis=1) == codes_k
            product = jnp.where(same, product, 0.0).reshape(TILES, 16, 256)
            acc[d] += jnp.sum(product, axis=0)
    norms_across = across[16:17] + across[17:18] + across[18:19]
    for d in range(len(chosen)):
        acc[d] = acc[d] / (piece_norms[d] + norms_across - acc[d])


def own_kernel(rows, own, out, row_codes, piece_codes):
    compare(rows, own, list(range(own.shape[0])), row_codes, piece_codes, out)


def other_kernel(
    kept, rows, early, late, early_ratio, late_ratio, out, row_codes, piece_codes, acc, tall, picked, own_ratio
):
    x, c = lax.axis_index("x"), lax.axis_index("c")
    core = c if kept else 1 - c
    odd = [4 * core + 1, 4 * core + 3, 4 * core + 9, 4 * core + 11]
    chosen = [(((u + 1) >> 1) - c) & 7 for u in odd]
    for d, place in enumerate(chosen):
        is_late = (place >> 1) == 2

        @pl.when(is_late)
        def _():
            picked[d] = late[place & 1]

        @pl.when(jnp.logical_not(is_late))
        def _():
            picked[d] = early[jnp.where(place > 3, place - 2, place)]

    for d in range(8):
        own_ratio[d] = late_ratio[d - 4] if d // 2 == 2 else early_ratio[EARLY.index(d)]
    compare(rows, picked, list(range(4)), row_codes, piece_codes, acc)
    low_lanes = lax.broadcasted_iota(jnp.int32, (32, LANES), 1) < 64
    for half in range(2):
        for i in range(5):
            if i % 2 == 0:
                part = own_ratio[(4 * half + 2 * core + i // 2) & 7]
            else:
                part = acc[2 * half + i // 2]
            tall[half, i * 16 : i * 16 + 16, :] = part
        wide = jnp.transpose(tall[half], (1, 0))
        for panel in range(4):
            ratio = wide[panel * 64 : panel * 64 + 64]
            ratio = jnp.where(panel < x, pltpu.roll(ratio, 112, 1), ratio)
            out[panel, half] = jnp.where(low_lanes, ratio[0:32], pltpu.roll(ratio[32:64], 64, 1))


def place_kernel(arrived, out, tall):
    x = lax.axis_index("x")
    take = lax.broadcasted_iota(jnp.int32, (256, 512), 0)
    give = lax.broadcasted_iota(jnp.int32, (256, 512), 1)
    base = ((take >> 4) & 7) * 64 + (take & 15) * 4 + (take >> 7)
    results = []
    for delta in range(4):
        xs = (x - delta) & 3
        total = jnp.zeros((32, 512), F32)
        for yh in range(2):
            shift = (base + 2 * yh == give).astype(BF16)
            block = jnp.concatenate([arrived[0, xs, yh], arrived[1, xs, yh]], axis=1)
            high = block.astype(BF16)
            rest = block - high.astype(F32)
            middle = rest.astype(BF16)
            low = (rest - middle.astype(F32)).astype(BF16)
            stacked = jnp.concatenate([high, middle, low], axis=0)
            moved = jnp.dot(stacked, shift, preferred_element_type=F32)
            total = total + ((moved[0:32] + moved[32:64]) + moved[64:96])
        results.append(total)
    low_lanes = lax.broadcasted_iota(jnp.int32, (32, LANES), 1) < 64
    for h in range(2):
        for pair in range(2):
            for t in range(4):
                place = h * 256 + (t // 2) * 128
                even = results[2 * pair][:, place : place + 128]
                odd = results[2 * pair + 1][:, place : place + 128]
                if t % 2 == 0:
                    block = jnp.where(low_lanes, even, pltpu.roll(odd, 64, 1))
                else:
                    block = jnp.where(low_lanes, pltpu.roll(even, 64, 1), odd)
                for s in range(2):
                    tall[2 * t + pair, pl.ds(2 * h + s, 16, stride=4), :] = block[s * 16 : s * 16 + 16]
    for group in range(8):
        out[:, group * 128 : group * 128 + 128] = tall[group]


def step(block, axis, distance):
    size = lax.axis_size(axis)
    return lax.ppermute(block, axis, [((i - distance) % size, i) for i in range(size)])


def on_device(tile_values, tile_ids, doc_tiles, row_counts):
    c = lax.axis_index("c")
    sending = pl.pallas_call(
        pack_kernel,
        out_shape=jax.ShapeDtypeStruct((64, SENT // 2, 2, LANES), BF16),
        in_specs=[ANY, ANY, ANY, ANY],
        out_specs=VMEM,
        scratch_shapes=[
            pltpu.SMEM((64,), jnp.int32),
            pltpu.SMEM((128,), jnp.int32),
            pltpu.VMEM((TILES, LANES), jnp.int32),
            pltpu.VMEM((128, TILES, LANES), BF16),
            pltpu.VMEM((128, LANES), F32),
            pltpu.SemaphoreType.DMA((4,)),
        ],
        compiler_params=params(60),
    )(row_counts, doc_tiles, tile_ids.T, tile_values)
    source = pl.pallas_call(
        source_kernel,
        out_shape=jax.ShapeDtypeStruct((16,), jnp.int32),
        in_specs=[SMEM],
        out_specs=SMEM,
        compiler_params=params(4),
        cost_estimate=pl.CostEstimate(flops=2**30, bytes_accessed=2**20, transcendentals=0),
    )(row_counts)
    arrived = lax.all_to_all(sending, ("z", "yl", "x"), 0, 0, tiled=True)
    piece, spread = pl.pallas_call(
        arrange_kernel,
        out_shape=(
            jax.ShapeDtypeStruct((PIECE, 16, LANES), BF16),
            jax.ShapeDtypeStruct((16, PIECE, 16, LANES), BF16),
        ),
        in_specs=[SMEM, VMEM],
        out_specs=(VMEM, VMEM),
        scratch_shapes=[pltpu.VMEM((16 * SENT, LANES), F32)],
        compiler_params=params(16),
    )(source, arrived)
    rows = lax.all_to_all(spread, ("x", "yh", "yl"), 0, 0, tiled=True)
    ring = [piece] + [None] * 7
    ring[1] = step(piece, "z", 1)
    ahead, behind = lax.optimization_barrier((piece, ring[1]))
    for distance in range(1, 4):
        behind, ahead = step(behind, "z", 1), step(ahead, "z", -1)
        ring[distance + 1], ring[8 - distance] = behind, ahead
    def compare_own(own):
        count = own.shape[0]
        return pl.pallas_call(
            own_kernel,
            out_shape=jax.ShapeDtypeStruct((count, 16, 256), F32),
            in_specs=[VMEM, VMEM],
            out_specs=VMEM,
            scratch_shapes=[pltpu.VMEM((256, LANES), F32), pltpu.VMEM((count, TILES, 16, LANES), F32)],
            compiler_params=params(32),
            cost_estimate=cost(count),
        )(rows, own)

    early = jnp.stack([ring[d] for d in EARLY])
    other_early = step(early, "c", 1)
    early_ratio = compare_own(early)
    early_ratio, *last = lax.optimization_barrier((early_ratio, *(ring[d] for d in LATE)))
    late = jnp.stack(last)
    other_late = step(late, "c", 1)
    late_ratio = compare_own(late)

    def finish(kept):
        return pl.pallas_call(
            functools.partial(other_kernel, kept),
            out_shape=jax.ShapeDtypeStruct((4, 2, 32, LANES), F32),
            in_specs=[VMEM] * 5,
            out_specs=VMEM,
            scratch_shapes=[
                pltpu.VMEM((256, LANES), F32),
                pltpu.VMEM((4, TILES, 16, LANES), F32),
                pltpu.VMEM((4, 16, 256), F32),
                pltpu.VMEM((2, LANES, 256), F32),
                pltpu.VMEM((4, PIECE, 16, LANES), BF16),
                pltpu.VMEM((8, 16, 256), F32),
            ],
            compiler_params=params(32),
            cost_estimate=cost(4),
        )(rows, other_early, other_late, early_ratio, late_ratio)

    swapped = step(finish(False), "c", 1)
    kept = finish(True)
    results = jnp.where(c == 0, jnp.stack([kept, swapped]), jnp.stack([swapped, kept]))
    results = lax.all_to_all(
        results.reshape(16, 32, LANES), ("yl", "x", "yh"), 0, 0, tiled=True
    ).reshape(2, 4, 2, 32, LANES)
    return pl.pallas_call(
        place_kernel,
        out_shape=jax.ShapeDtypeStruct((64, 1024), F32),
        in_specs=[VMEM],
        out_specs=VMEM,
        scratch_shapes=[pltpu.VMEM((8, 64, LANES), F32)],
        compiler_params=params(16),
    )(results)


def solution(mesh):
    fine = Mesh(mesh.devices.reshape(8, 2, 4, 2, 2), ("z", "yl", "x", "yh", "c"))
    rows, columns = ("z", "yl", "x"), ("yh", "c")
    placed = (P(rows, None, None), P(rows, None), P(rows), P())
    return jax.shard_map(
        on_device, mesh=fine, in_specs=placed, out_specs=P(rows, columns), check_vma=False
    )
```

```python
import functools

import jax
import jax.numpy as jnp
from jax import lax
from jax.experimental import pallas as pl
from jax.experimental.pallas import tpu as pltpu
from jax.sharding import Mesh
from jax.sharding import PartitionSpec as P

TILES = 16
LANES = 128
SENT = 18
PIECE = TILES + 1
EARLY, LATE = (0, 1, 2, 3, 6, 7), (4, 5)
BF16 = jnp.bfloat16
F32 = jnp.float32
VMEM = pl.BlockSpec(memory_space=pltpu.VMEM)
ANY = pl.BlockSpec(memory_space=pl.ANY)
SMEM = pl.BlockSpec(memory_space=pltpu.SMEM)


def cost(pieces):
    return pl.CostEstimate(flops=2 * 4096 * 256 * pieces * LANES, bytes_accessed=2**21, transcendentals=0)


def params(mib):
    return pltpu.CompilerParams(vmem_limit_bytes=mib * 2**20)


def source_kernel(counts, source):
    z, yl, x = lax.axis_index("z"), lax.axis_index("yl"), lax.axis_index("x")
    yh, c = lax.axis_index("yh"), lax.axis_index("c")
    base = (yh * 2 + yl) * 64 + z * 8 + c * 4 + x

    def scan(e, begin):
        end = begin + counts[e]
        number = begin + ((base - begin) & 255)

        @pl.when(number < end)
        def _():
            source[number >> 8] = (e & 3) * 16 + (e >> 3) * 2 + ((e >> 2) & 1)

        return end

    lax.fori_loop(0, 64, scan, jnp.int32(0), unroll=8)


def pack_kernel(counts_in, tiles_in, ids_in, values_in, out, counts, tiles, ids, values, wide_ids, sems):
    moves = [
        pltpu.make_async_copy(counts_in, counts, sems.at[0]),
        pltpu.make_async_copy(ids_in, ids, sems.at[1]),
        pltpu.make_async_copy(tiles_in, tiles, sems.at[2]),
        pltpu.make_async_copy(values_in, values, sems.at[3]),
    ]
    for move in moves:
        move.start()
    yh, c = lax.axis_index("yh"), lax.axis_index("c")
    here = lax.axis_index("z") * 8 + lax.axis_index("yl") * 4 + lax.axis_index("x")
    moves[0].wait()
    own_begin = lax.fori_loop(
        0, 64, lambda e, begin: begin + jnp.where(e < here, counts[e], 0), jnp.int32(0), unroll=16
    )
    moves[1].wait()
    tall_ids = jnp.concatenate([ids[...].astype(F32), jnp.zeros((LANES - TILES, LANES), F32)], axis=0)
    wide_ids[...] = jnp.transpose(tall_ids, (1, 0))
    moves[2].wait()
    moves[3].wait()
    tile_line = lax.broadcasted_iota(jnp.int32, (TILES, LANES), 0)

    def fill(t, carry):
        wanted = (yh * 2 + (t & 1)) * 64 + ((t >> 1) & 7) * 8 + c * 4 + (t >> 4)
        slot = jnp.minimum((wanted - own_begin) & 255, 127)
        document = jnp.where(tile_line < tiles[slot], values[slot].astype(F32), 0.0)
        codes = jnp.broadcast_to(wide_ids[pl.ds(slot, 1), :], (SENT - TILES, LANES))
        whole = jnp.concatenate([document, codes], axis=0).astype(BF16)
        out[t] = whole.reshape(SENT // 2, 2, LANES)
        return carry

    lax.fori_loop(0, 64, fill, 0, unroll=8)


def arrange_kernel(source, arrived, piece, spread, lines):
    for m in range(16):
        lines[pl.ds(m * SENT, SENT), :] = arrived[source[m]].reshape(SENT, LANES).astype(F32)
    total = jnp.zeros((16, LANES), F32)
    parts = []
    for k in range(TILES):
        part = lines[pl.ds(k, 16, stride=SENT), :]
        total = total + part * part
        parts.append(part.astype(BF16))
    norms = jnp.sum(total, axis=1, keepdims=True)
    high = norms.astype(BF16).astype(F32)
    middle = (norms - high).astype(BF16).astype(F32)
    low = norms - high - middle
    lane = lax.broadcasted_iota(jnp.int32, (16, LANES), 1)
    codes = lines[pl.ds(TILES, 16, stride=SENT), :]
    codes = jnp.where(lane == 16, high, codes)
    codes = jnp.where(lane == 17, middle, codes)
    codes = jnp.where(lane == 18, low, codes)
    parts.append(codes.astype(BF16))
    whole = jnp.concatenate([part[None] for part in parts], axis=0)
    piece[...] = whole
    for j in range(16):
        spread[j] = whole


def compare(rows, pieces, chosen, row_codes, piece_codes, acc):
    for j in range(16):
        row_codes[j * 16 : j * 16 + 16, :] = rows[j, TILES].astype(F32)
    across = jnp.transpose(row_codes[...], (1, 0))
    row_codes[0:128, :] = across[:, 0:128]
    row_codes[128:256, :] = across[:, 128:256]
    piece_norms = []
    for d, place in enumerate(chosen):
        codes = pieces[place, TILES].astype(F32)
        for k in range(TILES):
            piece_codes[d, k] = jnp.broadcast_to(codes[:, k : k + 1], (16, LANES))
        norms = codes[:, 16:17] + codes[:, 17:18] + codes[:, 18:19]
        piece_norms.append(jnp.broadcast_to(norms, (16, 256)))
    acc[...] = jnp.zeros_like(acc)
    for k in range(TILES):
        weights = jnp.transpose(rows[:, k].reshape(256, LANES), (1, 0))
        codes_k = jnp.concatenate(
            [row_codes[pl.ds(k, 1), :], row_codes[pl.ds(128 + k, 1), :]], axis=1
        )
        for d, place in enumerate(chosen):
            left = pieces[place, 0:TILES].reshape(256, LANES)
            product = jnp.dot(left, weights, preferred_element_type=F32)
            codes_d = piece_codes[d].reshape(256, LANES)
            same = jnp.concatenate([codes_d, codes_d], axis=1) == codes_k
            product = jnp.where(same, product, 0.0).reshape(TILES, 16, 256)
            acc[d] += jnp.sum(product, axis=0)
    norms_across = across[16:17] + across[17:18] + across[18:19]
    for d in range(len(chosen)):
        acc[d] = acc[d] / (piece_norms[d] + norms_across - acc[d])


def own_kernel(rows, own, out, row_codes, piece_codes):
    compare(rows, own, list(range(own.shape[0])), row_codes, piece_codes, out)


def other_kernel(
    kept, rows, early, late, early_ratio, late_ratio, out, row_codes, piece_codes, acc, tall, picked, own_ratio
):
    x, c = lax.axis_index("x"), lax.axis_index("c")
    core = c if kept else 1 - c
    odd = [4 * core + 1, 4 * core + 3, 4 * core + 9, 4 * core + 11]
    chosen = [(((u + 1) >> 1) - c) & 7 for u in odd]
    for d, place in enumerate(chosen):
        is_late = (place >> 1) == 2

        @pl.when(is_late)
        def _():
            picked[d] = late[place & 1]

        @pl.when(jnp.logical_not(is_late))
        def _():
            picked[d] = early[jnp.where(place > 3, place - 2, place)]

    for d in range(8):
        own_ratio[d] = late_ratio[d - 4] if d // 2 == 2 else early_ratio[EARLY.index(d)]
    compare(rows, picked, list(range(4)), row_codes, piece_codes, acc)
    low_lanes = lax.broadcasted_iota(jnp.int32, (32, LANES), 1) < 64
    for half in range(2):
        for i in range(5):
            if i % 2 == 0:
                part = own_ratio[(4 * half + 2 * core + i // 2) & 7]
            else:
                part = acc[2 * half + i // 2]
            tall[half, i * 16 : i * 16 + 16, :] = part
        wide = jnp.transpose(tall[half], (1, 0))
        for panel in range(4):
            ratio = wide[panel * 64 : panel * 64 + 64]
            ratio = jnp.where(panel < x, pltpu.roll(ratio, 112, 1), ratio)
            out[panel, half] = jnp.where(low_lanes, ratio[0:32], pltpu.roll(ratio[32:64], 64, 1))


def place_kernel(arrived, out, tall):
    x = lax.axis_index("x")
    take = lax.broadcasted_iota(jnp.int32, (256, 512), 0)
    give = lax.broadcasted_iota(jnp.int32, (256, 512), 1)
    base = ((take >> 4) & 7) * 64 + (take & 15) * 4 + (take >> 7)
    results = []
    for delta in range(4):
        xs = (x - delta) & 3
        total = jnp.zeros((32, 512), F32)
        for yh in range(2):
            shift = (base + 2 * yh == give).astype(BF16)
            block = jnp.concatenate([arrived[0, xs, yh], arrived[1, xs, yh]], axis=1)
            high = block.astype(BF16)
            rest = block - high.astype(F32)
            middle = rest.astype(BF16)
            low = (rest - middle.astype(F32)).astype(BF16)
            stacked = jnp.concatenate([high, middle, low], axis=0)
            moved = jnp.dot(stacked, shift, preferred_element_type=F32)
            total = total + ((moved[0:32] + moved[32:64]) + moved[64:96])
        results.append(total)
    low_lanes = lax.broadcasted_iota(jnp.int32, (32, LANES), 1) < 64
    for h in range(2):
        for pair in range(2):
            for t in range(4):
                place = h * 256 + (t // 2) * 128
                even = results[2 * pair][:, place : place + 128]
                odd = results[2 * pair + 1][:, place : place + 128]
                if t % 2 == 0:
                    block = jnp.where(low_lanes, even, pltpu.roll(odd, 64, 1))
                else:
                    block = jnp.where(low_lanes, pltpu.roll(even, 64, 1), odd)
                for s in range(2):
                    tall[2 * t + pair, pl.ds(2 * h + s, 16, stride=4), :] = block[s * 16 : s * 16 + 16]
    for group in range(8):
        out[:, group * 128 : group * 128 + 128] = tall[group]


def step(block, axis, distance):
    size = lax.axis_size(axis)
    return lax.ppermute(block, axis, [((i - distance) % size, i) for i in range(size)])


def on_device(tile_values, tile_ids, doc_tiles, row_counts):
    c = lax.axis_index("c")
    sending = pl.pallas_call(
        pack_kernel,
        out_shape=jax.ShapeDtypeStruct((64, SENT // 2, 2, LANES), BF16),
        in_specs=[ANY, ANY, ANY, ANY],
        out_specs=VMEM,
        scratch_shapes=[
            pltpu.SMEM((64,), jnp.int32),
            pltpu.SMEM((128,), jnp.int32),
            pltpu.VMEM((TILES, LANES), jnp.int32),
            pltpu.VMEM((128, TILES, LANES), BF16),
            pltpu.VMEM((128, LANES), F32),
            pltpu.SemaphoreType.DMA((4,)),
        ],
        compiler_params=params(60),
    )(row_counts, doc_tiles, tile_ids.T, tile_values)
    source = pl.pallas_call(
        source_kernel,
        out_shape=jax.ShapeDtypeStruct((16,), jnp.int32),
        in_specs=[SMEM],
        out_specs=SMEM,
        compiler_params=params(4),
        cost_estimate=pl.CostEstimate(flops=2**30, bytes_accessed=2**20, transcendentals=0),
    )(row_counts)
    arrived = lax.all_to_all(sending, ("x", "z", "yl"), 0, 0, tiled=True)
    piece, spread = pl.pallas_call(
        arrange_kernel,
        out_shape=(
            jax.ShapeDtypeStruct((PIECE, 16, LANES), BF16),
            jax.ShapeDtypeStruct((16, PIECE, 16, LANES), BF16),
        ),
        in_specs=[SMEM, VMEM],
        out_specs=(VMEM, VMEM),
        scratch_shapes=[pltpu.VMEM((16 * SENT, LANES), F32)],
        compiler_params=params(16),
    )(source, arrived)
    rows = lax.all_to_all(spread, ("x", "yh", "yl"), 0, 0, tiled=True)
    ring = [piece] + [None] * 7
    ring[1] = step(piece, "z", 1)
    ahead, behind = lax.optimization_barrier((piece, ring[1]))
    for distance in range(1, 4):
        behind, ahead = step(behind, "z", 1), step(ahead, "z", -1)
        ring[distance + 1], ring[8 - distance] = behind, ahead
    def compare_own(own):
        count = own.shape[0]
        return pl.pallas_call(
            own_kernel,
            out_shape=jax.ShapeDtypeStruct((count, 16, 256), F32),
            in_specs=[VMEM, VMEM],
            out_specs=VMEM,
            scratch_shapes=[pltpu.VMEM((256, LANES), F32), pltpu.VMEM((count, TILES, 16, LANES), F32)],
            compiler_params=params(32),
            cost_estimate=cost(count),
        )(rows, own)

    early = jnp.stack([ring[d] for d in EARLY])
    other_early = step(early, "c", 1)
    early_ratio = compare_own(early)
    early_ratio, *last = lax.optimization_barrier((early_ratio, *(ring[d] for d in LATE)))
    late = jnp.stack(last)
    other_late = step(late, "c", 1)
    late_ratio = compare_own(late)

    def finish(kept):
        return pl.pallas_call(
            functools.partial(other_kernel, kept),
            out_shape=jax.ShapeDtypeStruct((4, 2, 32, LANES), F32),
            in_specs=[VMEM] * 5,
            out_specs=VMEM,
            scratch_shapes=[
                pltpu.VMEM((256, LANES), F32),
                pltpu.VMEM((4, TILES, 16, LANES), F32),
                pltpu.VMEM((4, 16, 256), F32),
                pltpu.VMEM((2, LANES, 256), F32),
                pltpu.VMEM((4, PIECE, 16, LANES), BF16),
                pltpu.VMEM((8, 16, 256), F32),
            ],
            compiler_params=params(32),
            cost_estimate=cost(4),
        )(rows, other_early, other_late, early_ratio, late_ratio)

    swapped = step(finish(False), "c", 1)
    kept = finish(True)
    results = jnp.where(c == 0, jnp.stack([kept, swapped]), jnp.stack([swapped, kept]))
    results = lax.all_to_all(
        results.reshape(16, 32, LANES), ("yl", "x", "yh"), 0, 0, tiled=True
    ).reshape(2, 4, 2, 32, LANES)
    return pl.pallas_call(
        place_kernel,
        out_shape=jax.ShapeDtypeStruct((64, 1024), F32),
        in_specs=[VMEM],
        out_specs=VMEM,
        scratch_shapes=[pltpu.VMEM((8, 64, LANES), F32)],
        compiler_params=params(16),
    )(results)


def solution(mesh):
    fine = Mesh(mesh.devices.reshape(8, 2, 4, 2, 2), ("z", "yl", "x", "yh", "c"))
    rows, columns = ("z", "yl", "x"), ("yh", "c")
    placed = (P(rows, None, None), P(rows, None), P(rows), P())
    return jax.shard_map(
        on_device, mesh=fine, in_specs=placed, out_specs=P(rows, columns), check_vma=False
    )
```

```python
import functools

import jax
import jax.numpy as jnp
from jax import lax
from jax.experimental import pallas as pl
from jax.experimental.pallas import tpu as pltpu
from jax.sharding import Mesh
from jax.sharding import PartitionSpec as P

TILES = 16
LANES = 128
SENT = 18
PIECE = TILES + 1
EARLY, LATE = (0, 1, 2, 3, 6, 7), (4, 5)
BF16 = jnp.bfloat16
F32 = jnp.float32
VMEM = pl.BlockSpec(memory_space=pltpu.VMEM)
ANY = pl.BlockSpec(memory_space=pl.ANY)
SMEM = pl.BlockSpec(memory_space=pltpu.SMEM)


def cost(pieces):
    return pl.CostEstimate(flops=2 * 4096 * 256 * pieces * LANES, bytes_accessed=2**21, transcendentals=0)


def params(mib):
    return pltpu.CompilerParams(vmem_limit_bytes=mib * 2**20)


def source_kernel(counts, source):
    z, yl, x = lax.axis_index("z"), lax.axis_index("yl"), lax.axis_index("x")
    yh, c = lax.axis_index("yh"), lax.axis_index("c")
    base = (yh * 2 + yl) * 64 + z * 8 + c * 4 + x

    def scan(e, begin):
        end = begin + counts[e]
        number = begin + ((base - begin) & 255)

        @pl.when(number < end)
        def _():
            source[number >> 8] = (e & 3) * 16 + (e >> 3) * 2 + ((e >> 2) & 1)

        return end

    lax.fori_loop(0, 64, scan, jnp.int32(0), unroll=8)


def pack_kernel(counts_in, tiles_in, ids_in, values_in, out, counts, tiles, ids, values, wide_ids, sems):
    moves = [
        pltpu.make_async_copy(counts_in, counts, sems.at[0]),
        pltpu.make_async_copy(ids_in, ids, sems.at[1]),
        pltpu.make_async_copy(tiles_in, tiles, sems.at[2]),
        pltpu.make_async_copy(values_in, values, sems.at[3]),
    ]
    for move in moves:
        move.start()
    yh, c = lax.axis_index("yh"), lax.axis_index("c")
    here = lax.axis_index("z") * 8 + lax.axis_index("yl") * 4 + lax.axis_index("x")
    moves[0].wait()
    own_begin = lax.fori_loop(
        0, 64, lambda e, begin: begin + jnp.where(e < here, counts[e], 0), jnp.int32(0), unroll=16
    )
    moves[1].wait()
    tall_ids = jnp.concatenate([ids[...].astype(F32), jnp.zeros((LANES - TILES, LANES), F32)], axis=0)
    wide_ids[...] = jnp.transpose(tall_ids, (1, 0))
    moves[2].wait()
    moves[3].wait()
    tile_line = lax.broadcasted_iota(jnp.int32, (TILES, LANES), 0)

    def fill(t, carry):
        wanted = (yh * 2 + (t & 1)) * 64 + ((t >> 1) & 7) * 8 + c * 4 + (t >> 4)
        slot = jnp.minimum((wanted - own_begin) & 255, 127)
        document = jnp.where(tile_line < tiles[slot], values[slot].astype(F32), 0.0)
        codes = jnp.broadcast_to(wide_ids[pl.ds(slot, 1), :], (SENT - TILES, LANES))
        whole = jnp.concatenate([document, codes], axis=0).astype(BF16)
        out[t] = whole.reshape(SENT // 2, 2, LANES)
        return carry

    lax.fori_loop(0, 64, fill, 0, unroll=8)


def arrange_kernel(source, arrived, piece, spread, lines):
    for m in range(16):
        lines[pl.ds(m * SENT, SENT), :] = arrived[source[m]].reshape(SENT, LANES).astype(F32)
    total = jnp.zeros((16, LANES), F32)
    parts = []
    for k in range(TILES):
        part = lines[pl.ds(k, 16, stride=SENT), :]
        total = total + part * part
        parts.append(part.astype(BF16))
    norms = jnp.sum(total, axis=1, keepdims=True)
    high = norms.astype(BF16).astype(F32)
    middle = (norms - high).astype(BF16).astype(F32)
    low = norms - high - middle
    lane = lax.broadcasted_iota(jnp.int32, (16, LANES), 1)
    codes = lines[pl.ds(TILES, 16, stride=SENT), :]
    codes = jnp.where(lane == 16, high, codes)
    codes = jnp.where(lane == 17, middle, codes)
    codes = jnp.where(lane == 18, low, codes)
    parts.append(codes.astype(BF16))
    whole = jnp.concatenate([part[None] for part in parts], axis=0)
    piece[...] = whole
    for j in range(16):
        spread[j] = whole


def compare(rows, pieces, chosen, row_codes, piece_codes, acc):
    piece_norms = []
    for d, place in enumerate(chosen):
        codes = pieces[place, TILES].astype(F32)
        for k in range(TILES):
            piece_codes[d, k] = jnp.broadcast_to(codes[:, k : k + 1], (16, LANES))
        norms = codes[:, 16:17] + codes[:, 17:18] + codes[:, 18:19]
        piece_norms.append(jnp.broadcast_to(norms, (16, 256)))
    acc[...] = jnp.zeros_like(acc)
    for k in range(TILES):
        weights = jnp.transpose(rows[:, k].reshape(256, LANES), (1, 0))
        codes_k = jnp.concatenate(
            [row_codes[pl.ds(k, 1), :], row_codes[pl.ds(128 + k, 1), :]], axis=1
        )
        for d, place in enumerate(chosen):
            left = pieces[place, 0:TILES].reshape(256, LANES)
            product = jnp.dot(left, weights, preferred_element_type=F32)
            codes_d = piece_codes[d].reshape(256, LANES)
            same = jnp.concatenate([codes_d, codes_d], axis=1) == codes_k
            product = jnp.where(same, product, 0.0).reshape(TILES, 16, 256)
            acc[d] += jnp.sum(product, axis=0)
    across = jnp.concatenate([row_codes[16:24, :], row_codes[144:152, :]], axis=1)
    norms_across = across[0:1] + across[1:2] + across[2:3]
    for d in range(len(chosen)):
        acc[d] = acc[d] / (piece_norms[d] + norms_across - acc[d])


def early_kernel(rows, own, out, row_codes, piece_codes):
    for j in range(16):
        row_codes[j * 16 : j * 16 + 16, :] = rows[j, TILES].astype(F32)
    across = jnp.transpose(row_codes[...], (1, 0))
    row_codes[0:128, :] = across[:, 0:128]
    row_codes[128:256, :] = across[:, 128:256]
    compare(rows, own, list(range(own.shape[0])), row_codes, piece_codes, out)


def late_kernel(rows, own, row_codes, out, piece_codes):
    compare(rows, own, list(range(own.shape[0])), row_codes, piece_codes, out)


def other_kernel(
    kept, rows, row_codes, early, late, early_ratio, late_ratio, out, piece_codes, acc, tall, picked, own_ratio
):
    x, c = lax.axis_index("x"), lax.axis_index("c")
    core = c if kept else 1 - c
    odd = [4 * core + 1, 4 * core + 3, 4 * core + 9, 4 * core + 11]
    chosen = [(((u + 1) >> 1) - c) & 7 for u in odd]
    for d, place in enumerate(chosen):
        is_late = (place >> 1) == 2

        @pl.when(is_late)
        def _():
            picked[d] = late[place & 1]

        @pl.when(jnp.logical_not(is_late))
        def _():
            picked[d] = early[jnp.where(place > 3, place - 2, place)]

    for d in range(8):
        own_ratio[d] = late_ratio[d - 4] if d // 2 == 2 else early_ratio[EARLY.index(d)]
    compare(rows, picked, list(range(4)), row_codes, piece_codes, acc)
    low_lanes = lax.broadcasted_iota(jnp.int32, (32, LANES), 1) < 64
    for half in range(2):
        for i in range(5):
            if i % 2 == 0:
                part = own_ratio[(4 * half + 2 * core + i // 2) & 7]
            else:
                part = acc[2 * half + i // 2]
            tall[half, i * 16 : i * 16 + 16, :] = part
        wide = jnp.transpose(tall[half], (1, 0))
        for panel in range(4):
            ratio = wide[panel * 64 : panel * 64 + 64]
            ratio = jnp.where(panel < x, pltpu.roll(ratio, 112, 1), ratio)
            out[panel, half] = jnp.where(low_lanes, ratio[0:32], pltpu.roll(ratio[32:64], 64, 1))


def place_kernel(arrived, out, tall):
    x = lax.axis_index("x")
    take = lax.broadcasted_iota(jnp.int32, (256, 512), 0)
    give = lax.broadcasted_iota(jnp.int32, (256, 512), 1)
    base = ((take >> 4) & 7) * 64 + (take & 15) * 4 + (take >> 7)
    results = []
    for delta in range(4):
        xs = (x - delta) & 3
        total = jnp.zeros((32, 512), F32)
        for yh in range(2):
            shift = (base + 2 * yh == give).astype(BF16)
            block = jnp.concatenate([arrived[xs, yh, 0], arrived[xs, yh, 1]], axis=1)
            high = block.astype(BF16)
            rest = block - high.astype(F32)
            middle = rest.astype(BF16)
            low = (rest - middle.astype(F32)).astype(BF16)
            stacked = jnp.concatenate([high, middle, low], axis=0)
            moved = jnp.dot(stacked, shift, preferred_element_type=F32)
            total = total + ((moved[0:32] + moved[32:64]) + moved[64:96])
        results.append(total)
    low_lanes = lax.broadcasted_iota(jnp.int32, (32, LANES), 1) < 64
    for h in range(2):
        for pair in range(2):
            for t in range(4):
                place = h * 256 + (t // 2) * 128
                even = results[2 * pair][:, place : place + 128]
                odd = results[2 * pair + 1][:, place : place + 128]
                if t % 2 == 0:
                    block = jnp.where(low_lanes, even, pltpu.roll(odd, 64, 1))
                else:
                    block = jnp.where(low_lanes, pltpu.roll(even, 64, 1), odd)
                for s in range(2):
                    tall[2 * t + pair, pl.ds(2 * h + s, 16, stride=4), :] = block[s * 16 : s * 16 + 16]
    for group in range(8):
        out[:, group * 128 : group * 128 + 128] = tall[group]


def step(block, axis, distance):
    size = lax.axis_size(axis)
    return lax.ppermute(block, axis, [((i - distance) % size, i) for i in range(size)])


def on_device(tile_values, tile_ids, doc_tiles, row_counts):
    c = lax.axis_index("c")
    sending = pl.pallas_call(
        pack_kernel,
        out_shape=jax.ShapeDtypeStruct((64, SENT // 2, 2, LANES), BF16),
        in_specs=[ANY, ANY, ANY, ANY],
        out_specs=VMEM,
        scratch_shapes=[
            pltpu.SMEM((64,), jnp.int32),
            pltpu.SMEM((128,), jnp.int32),
            pltpu.VMEM((TILES, LANES), jnp.int32),
            pltpu.VMEM((128, TILES, LANES), BF16),
            pltpu.VMEM((128, LANES), F32),
            pltpu.SemaphoreType.DMA((4,)),
        ],
        compiler_params=params(60),
    )(row_counts, doc_tiles, tile_ids.T, tile_values)
    source = pl.pallas_call(
        source_kernel,
        out_shape=jax.ShapeDtypeStruct((16,), jnp.int32),
        in_specs=[SMEM],
        out_specs=SMEM,
        compiler_params=params(4),
        cost_estimate=pl.CostEstimate(flops=2**30, bytes_accessed=2**20, transcendentals=0),
    )(row_counts)
    arrived = lax.all_to_all(sending, ("x", "z", "yl"), 0, 0, tiled=True)
    piece, spread = pl.pallas_call(
        arrange_kernel,
        out_shape=(
            jax.ShapeDtypeStruct((PIECE, 16, LANES), BF16),
            jax.ShapeDtypeStruct((16, PIECE, 16, LANES), BF16),
        ),
        in_specs=[SMEM, VMEM],
        out_specs=(VMEM, VMEM),
        scratch_shapes=[pltpu.VMEM((16 * SENT, LANES), F32)],
        compiler_params=params(16),
    )(source, arrived)
    rows = lax.all_to_all(spread, ("x", "yh", "yl"), 0, 0, tiled=True)
    ring = [piece] + [None] * 7
    ring[1] = step(piece, "z", 1)
    ahead, behind = lax.optimization_barrier((piece, ring[1]))
    for distance in range(1, 4):
        behind, ahead = step(behind, "z", 1), step(ahead, "z", -1)
        ring[distance + 1], ring[8 - distance] = behind, ahead
    early = jnp.stack([ring[d] for d in EARLY])
    other_early = step(early, "c", 1)
    early_ratio, row_codes = pl.pallas_call(
        early_kernel,
        out_shape=(
            jax.ShapeDtypeStruct((len(EARLY), 16, 256), F32),
            jax.ShapeDtypeStruct((256, LANES), F32),
        ),
        in_specs=[VMEM, VMEM],
        out_specs=(VMEM, VMEM),
        scratch_shapes=[pltpu.VMEM((len(EARLY), TILES, 16, LANES), F32)],
        compiler_params=params(32),
        cost_estimate=cost(len(EARLY)),
    )(rows, early)
    early_ratio, *last = lax.optimization_barrier((early_ratio, *(ring[d] for d in LATE)))
    late = jnp.stack(last)
    other_late = step(late, "c", 1)
    late_ratio = pl.pallas_call(
        late_kernel,
        out_shape=jax.ShapeDtypeStruct((len(LATE), 16, 256), F32),
        in_specs=[VMEM, VMEM, VMEM],
        out_specs=VMEM,
        scratch_shapes=[pltpu.VMEM((len(LATE), TILES, 16, LANES), F32)],
        compiler_params=params(32),
        cost_estimate=cost(len(LATE)),
    )(rows, late, row_codes)

    def finish(kept):
        return pl.pallas_call(
            functools.partial(other_kernel, kept),
            out_shape=jax.ShapeDtypeStruct((4, 2, 32, LANES), F32),
            in_specs=[VMEM] * 6,
            out_specs=VMEM,
            scratch_shapes=[
                pltpu.VMEM((4, TILES, 16, LANES), F32),
                pltpu.VMEM((4, 16, 256), F32),
                pltpu.VMEM((2, LANES, 256), F32),
                pltpu.VMEM((4, PIECE, 16, LANES), BF16),
                pltpu.VMEM((8, 16, 256), F32),
            ],
            compiler_params=params(32),
            cost_estimate=cost(4),
        )(rows, row_codes, other_early, other_late, early_ratio, late_ratio)

    swapped = step(finish(False), "c", 1)
    kept = finish(True)
    results = jnp.where(c == 0, jnp.stack([kept, swapped], 2), jnp.stack([swapped, kept], 2))
    results = lax.all_to_all(
        results.reshape(16, 32, LANES), ("x", "yh", "yl"), 0, 0, tiled=True
    ).reshape(4, 2, 2, 32, LANES)
    return pl.pallas_call(
        place_kernel,
        out_shape=jax.ShapeDtypeStruct((64, 1024), F32),
        in_specs=[VMEM],
        out_specs=VMEM,
        scratch_shapes=[pltpu.VMEM((8, 64, LANES), F32)],
        compiler_params=params(16),
    )(results)


def solution(mesh):
    fine = Mesh(mesh.devices.reshape(8, 2, 4, 2, 2), ("z", "yl", "x", "yh", "c"))
    rows, columns = ("z", "yl", "x"), ("yh", "c")
    placed = (P(rows, None, None), P(rows, None), P(rows), P())
    return jax.shard_map(
        on_device, mesh=fine, in_specs=placed, out_specs=P(rows, columns), check_vma=False
    )
```
